32 devices in a mesh: dp: 4 (over y, core), mp: 8 (over z, x).
Axes of the slice: x: 2, y: 2, z: 4, core: 2. Of those that a mesh axis runs over, the one named last changes fastest.
Arguments:
- tokens_in: bfloat16 [128, 8192], P('dp'), may hold values from -6 to 6
- gate_pre: bfloat16 [128, 28672], P('dp', 'mp'), may hold values from -6 to 6
- up_pre: bfloat16 [128, 28672], P('dp', 'mp'), may hold values from -6 to 6
- down_weight: bfloat16 [28672, 8192], P('mp', 'dp'), may hold values from -0.03125 to 0.03125
- slot_source: int32 [128], replicated, may hold values from 0 to 127, each once
- encoder: bfloat16 [8192, 32768], P('dp', 'mp'), may hold values from -0.0625 to 0.0625
- encoder_bias: float32 [32768], P('mp'), may hold values from -3 to 3
- decoder: bfloat16 [32768, 8192], P('mp', 'dp'), may hold values from -0.03125 to 0.03125
- decoder_bias: float32 [8192], P('dp'), may hold values from -3 to 3
Outputs:
- activations: bfloat16 [128, 32768], P('dp', 'mp')
- code_grad: float32 [128, 32768], P('dp', 'mp')
- decoder_grad: float32 [32768, 8192], P('mp', 'dp')
The draws below stay inside these ranges and needn't reach their ends.
Inputs may be any that keep to these rules, and one draw needn't show every extreme that they name: Slot s of the shuffled batch takes harvested row slot_source[s]; every row fills exactly one slot.
All inputs are finite; a program needn't handle non-finite values.
Results may differ from the reference program's by a relative error of at most 0.015.
Values may be sent and summed in bfloat16 or wider, within the bound.
A program may use at most 192 MiB of HBM per device.

```python
import jax
import jax.numpy as jnp

D = 8192
FF = 28672
F = 32768
TOK_DEV = 32
TOKENS = 128


def level_of(key, dims, cuts, least, high):
    loudness = 1.0
    for position, shards_of in cuts:
        steps = jax.random.uniform(jax.random.fold_in(jax.random.fold_in(key, 6), position), (shards_of,), jnp.float32, least / len(cuts), high / len(cuts))
        loudness = loudness * jnp.repeat(jnp.exp(steps), dims[position] // shards_of).reshape((-1,) + (1,) * (len(dims) - 1 - position))
    return loudness


def gaussian(key, extent, spread, bound, shards=(), kind=jnp.bfloat16):
    drawn = jax.random.normal(key, extent, jnp.float32) * spread
    if len(shards) > 0:
        drawn = level_of(key, extent, shards, -0.22, 0.18) * drawn
    return jnp.clip(drawn, min=-bound, max=bound).astype(kind)


def setup_inputs(seed: int = 0) -> dict:
    arg_keys = jax.random.split(jax.random.key(seed), 10)
    tokens_in = gaussian(arg_keys[0], (TOKENS, D), 1.0, 6.0, ((0, 4),))
    gate_pre = gaussian(arg_keys[1], (TOKENS, FF), 1.0, 6.0, ((0, 4), (1, 8)))
    up_pre = gaussian(arg_keys[2], (TOKENS, FF), 1.0, 6.0, ((0, 4), (1, 8)))
    down_weight = gaussian(arg_keys[3], (FF, D), FF ** -0.5, 0.03125, ((0, 8), (1, 4)))
    slot_source = jax.random.permutation(arg_keys[4], TOKENS).astype(jnp.int32)
    encoder = gaussian(arg_keys[5], (D, F), D ** -0.5, 0.0625, ((0, 4), (1, 8)))
    encoder_bias = gaussian(arg_keys[6], (F,), 0.5, 3.0, ((0, 8),), jnp.float32)
    decoder = gaussian(arg_keys[7], (F, D), F ** -0.5, 0.03125, ((0, 8), (1, 4)))
    decoder_bias = gaussian(arg_keys[8], (D,), 0.5, 3.0, ((0, 4),), jnp.float32)
    return {"tokens_in": tokens_in, "gate_pre": gate_pre, "up_pre": up_pre, "down_weight": down_weight, "slot_source": slot_source, "encoder": encoder, "encoder_bias": encoder_bias, "decoder": decoder, "decoder_bias": decoder_bias}


def reference(tokens_in, gate_pre, up_pre, down_weight, slot_source, encoder, encoder_bias, decoder, decoder_bias):
    hidden = (jax.nn.silu(gate_pre.astype(jnp.float32)) * up_pre.astype(jnp.float32)).astype(jnp.bfloat16)
    target = jnp.dot(hidden, down_weight, preferred_element_type=jnp.float32)
    inputs = jnp.take(tokens_in, slot_source, axis=0)
    shuffled = jnp.take(target, slot_source, axis=0)
    preact = jnp.dot(inputs, encoder, preferred_element_type=jnp.float32) + encoder_bias
    all_codes = jnp.maximum(preact, 0.0).astype(jnp.bfloat16)
    rebuilt = jnp.dot(all_codes, decoder, preferred_element_type=jnp.float32) + decoder_bias
    residual_grad = (rebuilt - shuffled).astype(jnp.bfloat16)
    code_grad = jnp.dot(residual_grad, decoder.T, preferred_element_type=jnp.float32)
    decoder_grad = jnp.dot(all_codes.T, residual_grad, preferred_element_type=jnp.float32) / TOK_DEV
    return all_codes, code_grad, decoder_grad
```

```python
import functools

import jax
import jax.numpy as jnp
from jax import lax
from jax.experimental import pallas as pl
from jax.experimental.pallas import tpu as pltpu
from jax.sharding import PartitionSpec as P

MESH = pl.DeviceIdType.MESH
F32 = jnp.float32
BF16 = jnp.bfloat16
MIB = 1 << 20
CHUNKS = 4
HALVES = 2


def forward(
    sizes,
    slot_ref,
    tok_ref,
    gate_ref,
    up_ref,
    down_hbm,
    enc_hbm,
    eb_ref,
    dec_hbm,
    db_ref,
    act_out,
    cg_out,
    codes_out,
    res_out,
    enc,
    dec,
    down,
    tok_in,
    x,
    hid,
    hperm,
    part,
    psend,
    crecv,
    ysend,
    yrecv,
    codes,
    acc,
    ssend,
    xrecv,
    zsum,
    zsend,
    zrecv,
    res,
    send_sem,
    recv_sem,
    local_sem,
):
    dp, pairs, inner, outer, rows_here, cw, sw, tile, stile = sizes
    rows = dp * rows_here
    width = acc.shape[1]
    r16 = rows // (inner * outer)
    d = lax.axis_index("dp")
    m = lax.axis_index("mp")
    q, c = d // 2, lax.rem(d, 2)
    b, a = m // inner, lax.rem(m, inner)
    partner = 2 * q + 1 - c

    counter = [0, 0]

    def send(src, dst, **where):
        i = counter[0]
        counter[0] += 1
        copy = pltpu.make_async_remote_copy(
            src_ref=src,
            dst_ref=dst,
            send_sem=send_sem.at[i],
            recv_sem=recv_sem.at[i],
            device_id=where,
            device_id_type=MESH,
        )
        copy.start()
        return copy

    def local(src, dst):
        i = counter[1]
        counter[1] += 1
        copy = pltpu.make_async_copy(src, dst, local_sem.at[i])
        copy.start()
        return copy

    def at_chunk(k):
        return pl.ds(k * cw, cw)

    tok_own = local(tok_ref.at[:, pl.ds(pl.multiple_of(d * width, 128), width)], tok_in.at[d])
    enc_loads = [local(enc_hbm.at[:, at_chunk(k)], enc.at[k]) for k in range(CHUNKS)]
    down_load = local(down_hbm, down)
    dec_loads = [local(dec_hbm.at[at_chunk(k)], dec.at[at_chunk(k)]) for k in range(CHUNKS)]

    barrier = pltpu.get_barrier_semaphore()
    for i in range(1, dp):
        pl.semaphore_signal(
            barrier, inc=1, device_id={"dp": lax.rem(d + i, dp)}, device_id_type=MESH
        )
    for i in range(1, inner):
        pl.semaphore_signal(
            barrier,
            inc=1,
            device_id={"mp": b * inner + lax.rem(a + i, inner)},
            device_id_type=MESH,
        )
    for i in range(1, outer):
        pl.semaphore_signal(
            barrier,
            inc=1,
            device_id={"mp": lax.rem(b + i, outer) * inner + a},
            device_id_type=MESH,
        )
    pl.semaphore_wait(barrier, dp - 1 + inner - 1 + outer - 1)

    def same_core(i):
        return 2 * lax.rem(q + i, pairs) + c

    def gather_start(here):
        far = [send(here.at[d], here.at[d], dp=same_core(i)) for i in range(1, pairs)]
        near = send(here.at[d], here.at[d], dp=partner)
        return far, near

    def gather_pass(here, far):
        passed = []
        for i, copy in enumerate(far, 1):
            copy.wait_recv()
            came = 2 * lax.rem(q + pairs - i, pairs) + c
            passed.append(send(here.at[came], here.at[came], dp=partner))
        return passed

    tok_copies = []
    for i in range(1, dp):
        peer = lax.rem(d + i, dp)
        cols = pl.ds(pl.multiple_of(peer * width, 128), width)
        tok_copies.append(send(tok_ref.at[:, cols], tok_in.at[d], dp=peer))
    gate = gate_ref[...].astype(F32)
    hid[d] = (gate / (1.0 + jnp.exp(-gate)) * up_ref[...].astype(F32)).astype(BF16)
    hid_far, hid_near = gather_start(hid)

    pick = (slot_ref[...] == lax.broadcasted_iota(jnp.int32, (rows, rows), 1)).astype(F32)
    pick = pick.astype(BF16)

    tok_own.wait()
    for copy in tok_copies:
        copy.wait_recv()
    x[...] = jnp.dot(pick, tok_in[...].reshape(rows, width), preferred_element_type=F32).astype(
        BF16
    )

    def part_store(k, cols, value):
        value = value.reshape(dp, rows_here, value.shape[1])
        part[k, :, :, cols] = value
        psend[k, :, :, :, cols] = value.astype(BF16).reshape((pairs, 2) + value.shape[1:])

    def encode(k):
        enc_loads[k].wait()

        @pl.loop(0, cw // tile)
        def _(t):
            cols = pl.ds(pl.multiple_of(t * tile, tile), tile)
            part_store(k, cols, jnp.dot(x[...], enc[k, :, cols], preferred_element_type=F32))

        return send(psend.at[k, :, 1 - c], crecv.at[k], dp=partner)

    def pair_sum(k, core_copy):
        core_copy.wait_recv()
        for j in range(pairs):
            total = part[k, 2 * j + c] + crecv[k, j].astype(F32)
            part[k, 2 * j + c] = total
            ysend[k, j] = total.astype(BF16)
        return [
            send(ysend.at[k, lax.rem(q + i, pairs)], yrecv.at[k, i - 1], dp=same_core(i))
            for i in range(1, pairs)
        ]

    def far_sum(k, far_copies):
        total = part[k, d]
        for i, copy in enumerate(far_copies):
            copy.wait_recv()
            total = total + yrecv[k, i].astype(F32)
        return total

    def activate(k, far_copies):
        codes[k, d] = jnp.maximum(far_sum(k, far_copies) + eb_ref[:, at_chunk(k)], 0.0).astype(
            BF16
        )
        outs.append(local(codes.at[k, d], act_out.at[:, at_chunk(k)]))
        return gather_start(codes.at[k])

    def decode(k, near, passed, cols):
        for copy in [near] + passed:
            copy.wait_recv()
        outs.append(local(codes.at[k], codes_out.at[k]))
        dec_loads[k].wait()

        @pl.loop(0, width // tile)
        def _(t):
            cols = pl.ds(pl.multiple_of(t * tile, tile), tile)
            acc[:, cols] += jnp.dot(
                codes[k].reshape(rows, cw), dec[at_chunk(k), cols], preferred_element_type=F32
            )

    outs, sends = [], []
    core, far, gathers = {}, {}, {}
    for k in range(CHUNKS):
        core[k] = encode(k)
        if k >= 1:
            far[k - 1] = pair_sum(k - 1, core[k - 1])
    far[CHUNKS - 1] = pair_sum(CHUNKS - 1, core[CHUNKS - 1])

    hid_passed = gather_pass(hid, hid_far)
    gathers[0] = activate(0, far[0])
    for copy in [hid_near] + hid_passed:
        copy.wait_recv()
    hperm[...] = jnp.dot(
        pick, hid[...].reshape(rows, hid.shape[2]), preferred_element_type=F32
    ).astype(BF16)
    down_load.wait()
    passes = {}
    steps = width // tile
    for k in range(CHUNKS):

        @pl.loop(k * steps // CHUNKS, (k + 1) * steps // CHUNKS)
        def _(t):
            cols = pl.ds(pl.multiple_of(t * tile, tile), tile)
            acc[:, cols] = -jnp.dot(hperm[...], down[:, cols], preferred_element_type=F32)

        if k + 1 < CHUNKS:
            gathers[k + 1] = activate(k + 1, far[k + 1])
        passes[k] = gather_pass(codes.at[k], gathers[k][0])
    for k in range(CHUNKS - 1):
        decode(k, gathers[k][1], passes[k], None)

    last = CHUNKS - 1
    for copy in [gathers[last][1]] + passes[last]:
        copy.wait_recv()
    outs.append(local(codes.at[last], codes_out.at[last]))
    dec_loads[last].wait()

    def split_sum(s):
        @pl.loop(0, sw // stile)
        def _(t):
            there = pl.ds(pl.multiple_of(t * stile, stile), stile)
            cols = pl.ds(pl.multiple_of(s * sw + t * stile, stile), stile)
            total = acc[:, cols] + jnp.dot(
                codes[last].reshape(rows, cw), dec[at_chunk(last), cols], preferred_element_type=F32
            )
            acc[:, cols] = total
            ssend[s, :, :, :, there] = total.astype(BF16).reshape(inner, outer, r16, stile)

        return [
            send(
                ssend.at[s, lax.rem(a + i, inner)],
                xrecv.at[s, i - 1],
                mp=b * inner + lax.rem(a + i, inner),
            )
            for i in range(1, inner)
        ]

    def inner_sum(s, copies):
        own = pl.ds(pl.multiple_of(a * (outer * r16), outer * r16), outer * r16)
        total = acc[own, s * sw : (s + 1) * sw].reshape(outer, r16, sw)
        for i, copy in enumerate(copies):
            copy.wait_recv()
            total = total + xrecv[s, i].astype(F32)
        zsum[s] = total
        zsend[s] = total.astype(BF16)
        return [
            send(
                zsend.at[s, lax.rem(b + i, outer)],
                zrecv.at[s, i - 1],
                mp=lax.rem(b + i, outer) * inner + a,
            )
            for i in range(1, outer)
        ]

    def outer_sum(s, copies):
        total = zsum[s, b]
        for i, copy in enumerate(copies):
            copy.wait_recv()
            total = total + zrecv[s, i].astype(F32)
        res[s, a, b] = (total + db_ref[:, s * sw : (s + 1) * sw]).astype(BF16)
        return [
            send(res.at[s, a, b], res.at[s, a, b], mp=lax.rem(b + i, outer) * inner + a)
            for i in range(1, outer)
        ]

    def inner_gather(s, copies):
        for copy in copies:
            copy.wait_recv()
        return [
            send(res.at[s, a], res.at[s, a], mp=b * inner + lax.rem(a + i, inner))
            for i in range(1, inner)
        ]

    first = [split_sum(s) for s in range(HALVES)]
    second = [inner_sum(s, first[s]) for s in range(HALVES)]
    third = [outer_sum(s, second[s]) for s in range(HALVES)]
    fourth = [inner_gather(s, third[s]) for s in range(HALVES)]

    for k in range(CHUNKS):
        for copy in [core[k]] + far[k]:
            copy.wait_send()
    back, back_far = {}, {}
    for s in range(HALVES):
        for copy in fourth[s]:
            copy.wait_recv()
        outs.append(local(res.at[s], res_out.at[s]))
        for k in range(CHUNKS):

            @pl.loop(0, cw // tile)
            def _(t):
                cols = pl.ds(pl.multiple_of(t * tile, tile), tile)
                hidden_rows = pl.ds(pl.multiple_of(k * cw + t * tile, tile), tile)
                value = lax.dot_general(
                    res[s].reshape(rows, sw),
                    dec[hidden_rows, s * sw : (s + 1) * sw],
                    (((1,), (1,)), ((), ())),
                    preferred_element_type=F32,
                )
                if s > 0:
                    value = value + part[k, :, :, cols].reshape(rows, tile)
                if s < HALVES - 1:
                    part[k, :, :, cols] = value.reshape(dp, rows_here, tile)
                else:
                    part_store(k, cols, value)

            if s == HALVES - 1:
                back[k] = send(psend.at[k, :, 1 - c], crecv.at[k], dp=partner)
                if k >= 1:
                    back_far[k - 1] = pair_sum(k - 1, back[k - 1])
    back_far[last] = pair_sum(last, back[last])
    for k in range(CHUNKS):
        cg_out[:, at_chunk(k)] = far_sum(k, back_far[k])

    for copy in tok_copies + hid_far + [hid_near] + hid_passed:
        copy.wait_send()
    for k in range(CHUNKS):
        for copy in gathers[k][0] + [gathers[k][1]] + passes[k] + [back[k]] + back_far[k]:
            copy.wait_send()
    for s in range(HALVES):
        for copy in first[s] + second[s] + third[s] + fourth[s]:
            copy.wait_send()
    for copy in outs:
        copy.wait()


def decoder_gradient(scale, codes_ref, res_ref, out_ref):
    rows = codes_ref.shape[0] * codes_ref.shape[1]
    columns = res_ref.shape[2]
    for s in range(res_ref.shape[0]):
        out_ref[:, s * columns : (s + 1) * columns] = (
            lax.dot_general(
                codes_ref[...].reshape(rows, codes_ref.shape[2]),
                res_ref[s],
                (((0,), (0,)), ((), ())),
                preferred_element_type=F32,
            )
            * scale
        )


def on_device(
    dp,
    mp,
    tokens_in,
    gate_pre,
    up_pre,
    down_weight,
    slot_source,
    encoder,
    encoder_bias,
    decoder,
    decoder_bias,
):
    rows_here = tokens_in.shape[0]
    rows = rows_here * dp
    width, features = encoder.shape
    units = down_weight.shape[0]
    pairs = dp // 2
    inner = 1 << ((mp.bit_length() - 1) // 2)
    outer = mp // inner
    r16 = rows // mp
    cw, sw = features // CHUNKS, width // HALVES
    tile, stile = min(256, cw, width), min(256, sw)
    far = max(pairs - 1, 1)
    copies = (dp - 1) + 2 * pairs - 1 + CHUNKS * (1 + pairs - 1 + 2 * pairs - 1)
    copies += HALVES * 2 * (inner - 1 + outer - 1) + CHUNKS * pairs
    locals_ = 1 + CHUNKS + 1 + CHUNKS + 2 * CHUNKS + HALVES
    vmem = pl.BlockSpec(memory_space=pltpu.VMEM)
    anywhere = pl.BlockSpec(memory_space=pl.ANY)
    local_codes, code_grad, codes, res = pl.pallas_call(
        functools.partial(
            forward, (dp, pairs, inner, outer, rows_here, cw, sw, tile, stile)
        ),
        out_shape=(
            jax.ShapeDtypeStruct((rows_here, features), BF16),
            jax.ShapeDtypeStruct((rows_here, features), F32),
            jax.ShapeDtypeStruct((CHUNKS, dp, rows_here, cw), BF16),
            jax.ShapeDtypeStruct((HALVES, inner, outer, r16, sw), BF16),
        ),
        in_specs=[vmem, anywhere, vmem, vmem, anywhere, anywhere, vmem, anywhere, vmem],
        out_specs=(anywhere, vmem, anywhere, anywhere),
        scratch_shapes=[
            pltpu.VMEM((CHUNKS, width, cw), BF16),
            pltpu.VMEM((features, width), BF16),
            pltpu.VMEM((units, width), BF16),
            pltpu.VMEM((dp, rows_here, width), BF16),
            pltpu.VMEM((rows, width), BF16),
            pltpu.VMEM((dp, rows_here, units), BF16),
            pltpu.VMEM((rows, units), BF16),
            pltpu.VMEM((CHUNKS, dp, rows_here, cw), F32),
            pltpu.VMEM((CHUNKS, pairs, 2, rows_here, cw), BF16),
            pltpu.VMEM((CHUNKS, pairs, rows_here, cw), BF16),
            pltpu.VMEM((CHUNKS, pairs, rows_here, cw), BF16),
            pltpu.VMEM((CHUNKS, far, rows_here, cw), BF16),
            pltpu.VMEM((CHUNKS, dp, rows_here, cw), BF16),
            pltpu.VMEM((rows, width), F32),
            pltpu.VMEM((HALVES, inner, outer, r16, sw), BF16),
            pltpu.VMEM((HALVES, max(inner - 1, 1), outer, r16, sw), BF16),
            pltpu.VMEM((HALVES, outer, r16, sw), F32),
            pltpu.VMEM((HALVES, outer, r16, sw), BF16),
            pltpu.VMEM((HALVES, max(outer - 1, 1), r16, sw), BF16),
            pltpu.VMEM((HALVES, inner, outer, r16, sw), BF16),
            pltpu.SemaphoreType.DMA((copies,)),
            pltpu.SemaphoreType.DMA((copies,)),
            pltpu.SemaphoreType.DMA((locals_,)),
        ],
        compiler_params=pltpu.CompilerParams(
            collective_id=0, has_side_effects=True, vmem_limit_bytes=62 * MIB
        ),
        cost_estimate=pl.CostEstimate(
            flops=2 * rows * width * (2 * features + units) + 2 * rows * width * features,
            bytes_accessed=2 * width * (2 * features + units),
            transcendentals=0,
        ),
        name="forward",
    )(
        slot_source.reshape(rows, 1),
        tokens_in,
        gate_pre,
        up_pre,
        down_weight,
        encoder,
        encoder_bias.reshape(1, features),
        decoder,
        decoder_bias.reshape(1, width),
    )

    block = min(256, cw)
    per = cw // block
    decoder_grad = pl.pallas_call(
        functools.partial(decoder_gradient, 1.0 / rows_here),
        grid=(features // block,),
        out_shape=jax.ShapeDtypeStruct((features, width), F32),
        in_specs=[
            pl.BlockSpec((None, dp, rows_here, block), lambda f: (f // per, 0, 0, f % per)),
            pl.BlockSpec((HALVES, rows, sw), lambda f: (0, 0, 0)),
        ],
        out_specs=pl.BlockSpec((block, width), lambda f: (f, 0)),
        compiler_params=pltpu.CompilerParams(vmem_limit_bytes=32 * MIB),
        cost_estimate=pl.CostEstimate(
            flops=2 * rows * width * features,
            bytes_accessed=4 * width * features,
            transcendentals=0,
        ),
        name="decoder_gradient",
    )(codes, res.reshape(HALVES, rows, sw))
    return (local_codes, code_grad, decoder_grad)


def solution(mesh):
    return jax.shard_map(
        functools.partial(on_device, mesh.shape["dp"], mesh.shape["mp"]),
        mesh=mesh,
        in_specs=(
            P("dp", None),
            P("dp", "mp"),
            P("dp", "mp"),
            P("mp", "dp"),
            P(),
            P("dp", "mp"),
            P("mp"),
            P("mp", "dp"),
            P("dp"),
        ),
        out_specs=(P("dp", "mp"), P("dp", "mp"), P("mp", "dp")),
        check_vma=False,
    )
```

```python
import functools

import jax
import jax.numpy as jnp
from jax import lax
from jax.experimental import pallas as pl
from jax.experimental.pallas import tpu as pltpu
from jax.sharding import PartitionSpec as P

MESH = pl.DeviceIdType.MESH
F32 = jnp.float32
BF16 = jnp.bfloat16
MIB = 1 << 20
CHUNKS = 4
QUARTERS = 4


def forward(
    sizes,
    slot_ref,
    tok_ref,
    gate_ref,
    up_ref,
    down_hbm,
    enc_hbm,
    eb_ref,
    dec_hbm,
    db_ref,
    cg_out,
    codes_out,
    res_out,
    enc,
    dec,
    down,
    tok_in,
    x,
    hid,
    hperm,
    part,
    psend,
    crecv,
    ysend,
    yrecv,
    codes,
    acc,
    ssend,
    xrecv,
    zsum,
    zsend,
    zrecv,
    res,
    send_sem,
    recv_sem,
    local_sem,
):
    dp, pairs, inner, outer, rows_here, cw, sw, tile, stile = sizes
    rows = dp * rows_here
    width = acc.shape[1]
    r16 = rows // (inner * outer)
    d = lax.axis_index("dp")
    m = lax.axis_index("mp")
    q, c = d // 2, lax.rem(d, 2)
    b, a = m // inner, lax.rem(m, inner)
    partner = 2 * q + 1 - c

    counter = [0, 0]

    def send(src, dst, **where):
        i = counter[0]
        counter[0] += 1
        copy = pltpu.make_async_remote_copy(
            src_ref=src,
            dst_ref=dst,
            send_sem=send_sem.at[i],
            recv_sem=recv_sem.at[i],
            device_id=where,
            device_id_type=MESH,
        )
        copy.start()
        return copy

    def local(src, dst):
        i = counter[1]
        counter[1] += 1
        copy = pltpu.make_async_copy(src, dst, local_sem.at[i])
        copy.start()
        return copy

    def at_chunk(k):
        return pl.ds(k * cw, cw)

    tok_own = local(tok_ref.at[:, pl.ds(pl.multiple_of(d * width, 128), width)], tok_in.at[d])
    enc_loads = [local(enc_hbm.at[:, at_chunk(k)], enc.at[k]) for k in range(CHUNKS)]
    down_load = local(down_hbm, down)
    dec_loads = [local(dec_hbm.at[at_chunk(k)], dec.at[at_chunk(k)]) for k in range(CHUNKS)]

    barrier = pltpu.get_barrier_semaphore()
    for i in range(1, dp):
        pl.semaphore_signal(
            barrier, inc=1, device_id={"dp": lax.rem(d + i, dp)}, device_id_type=MESH
        )
    for i in range(1, inner):
        pl.semaphore_signal(
            barrier,
            inc=1,
            device_id={"mp": b * inner + lax.rem(a + i, inner)},
            device_id_type=MESH,
        )
    for i in range(1, outer):
        pl.semaphore_signal(
            barrier,
            inc=1,
            device_id={"mp": lax.rem(b + i, outer) * inner + a},
            device_id_type=MESH,
        )
    pl.semaphore_wait(barrier, dp - 1 + inner - 1 + outer - 1)

    def same_core(i):
        return 2 * lax.rem(q + i, pairs) + c

    def gather_start(here):
        far = [send(here.at[d], here.at[d], dp=same_core(i)) for i in range(1, pairs)]
        near = send(here.at[d], here.at[d], dp=partner)
        return far, near

    def gather_pass(here, far):
        passed = []
        for i, copy in enumerate(far, 1):
            copy.wait_recv()
            came = 2 * lax.rem(q + pairs - i, pairs) + c
            passed.append(send(here.at[came], here.at[came], dp=partner))
        return passed

    share = width // inner
    mine = pl.ds(pl.multiple_of(a * share, 128), share)
    cols = pl.ds(pl.multiple_of(partner * width, 128), width)
    tok_far = []
    for i in range(1, pairs):
        for j in range(2):
            core_there = lax.rem(c + j, 2)
            peer = 2 * lax.rem(q + i, pairs) + core_there
            came = 2 * lax.rem(q + pairs - i, pairs) + core_there
            there = pl.ds(pl.multiple_of(peer * width + a * share, 128), share)
            copy = send(tok_ref.at[:, there], tok_in.at[d, :, mine], dp=peer)
            tok_far.append((came, copy))
    tok_near = [send(tok_ref.at[:, cols], tok_in.at[d], dp=partner)]
    gate = gate_ref[...].astype(F32)
    hid[d] = (gate / (1.0 + jnp.exp(-gate)) * up_ref[...].astype(F32)).astype(BF16)
    hid_far, hid_near = gather_start(hid)

    pick = (slot_ref[...] == lax.broadcasted_iota(jnp.int32, (rows, rows), 0)).astype(F32)
    pick = pick.astype(BF16).T

    for came, copy in tok_far:
        copy.wait_recv()
        for i in range(1, inner):
            piece = tok_in.at[came, :, mine]
            tok_near.append(send(piece, piece, mp=b * inner + lax.rem(a + i, inner)))
    tok_own.wait()
    for copy in tok_near:
        copy.wait_recv()
    tok_copies = tok_near + [copy for _, copy in tok_far]
    x[...] = jnp.dot(pick, tok_in[...].reshape(rows, width), preferred_element_type=F32).astype(
        BF16
    )

    def part_store(k, cols, value):
        value = value.reshape(dp, rows_here, value.shape[1])
        part[k, :, :, cols] = value
        psend[k, :, :, :, cols] = value.astype(BF16).reshape((pairs, 2) + value.shape[1:])

    def encode(k):
        enc_loads[k].wait()

        @pl.loop(0, cw // tile)
        def _(t):
            cols = pl.ds(pl.multiple_of(t * tile, tile), tile)
            part_store(k, cols, jnp.dot(x[...], enc[k, :, cols], preferred_element_type=F32))

        return send(psend.at[k, :, 1 - c], crecv.at[k], dp=partner)

    def pair_sum(k, core_copy):
        core_copy.wait_recv()
        for j in range(pairs):
            total = part[k, 2 * j + c] + crecv[k, j].astype(F32)
            part[k, 2 * j + c] = total
            ysend[k, j] = total.astype(BF16)
        return [
            send(ysend.at[k, lax.rem(q + i, pairs)], yrecv.at[k, i - 1], dp=same_core(i))
            for i in range(1, pairs)
        ]

    def far_sum(k, far_copies):
        total = part[k, d]
        for i, copy in enumerate(far_copies):
            copy.wait_recv()
            total = total + yrecv[k, i].astype(F32)
        return total

    def activate(k, far_copies):
        codes[k, d] = jnp.maximum(far_sum(k, far_copies) + eb_ref[:, at_chunk(k)], 0.0).astype(
            BF16
        )
        return gather_start(codes.at[k])

    def decode(k, near, passed, cols):
        for copy in [near] + passed:
            copy.wait_recv()
        outs.append(local(codes.at[k], codes_out.at[k]))
        dec_loads[k].wait()

        @pl.loop(0, width // tile)
        def _(t):
            cols = pl.ds(pl.multiple_of(t * tile, tile), tile)
            acc[:, cols] += jnp.dot(
                codes[k].reshape(rows, cw), dec[at_chunk(k), cols], preferred_element_type=F32
            )

    outs, sends = [], []
    core, far, gathers = {}, {}, {}
    for k in range(CHUNKS):
        core[k] = encode(k)
        if k >= 1:
            far[k - 1] = pair_sum(k - 1, core[k - 1])
    far[CHUNKS - 1] = pair_sum(CHUNKS - 1, core[CHUNKS - 1])

    hid_passed = gather_pass(hid, hid_far)
    gathers[0] = activate(0, far[0])
    for copy in [hid_near] + hid_passed:
        copy.wait_recv()
    hperm[...] = jnp.dot(
        pick, hid[...].reshape(rows, hid.shape[2]), preferred_element_type=F32
    ).astype(BF16)
    down_load.wait()
    passes = {}
    steps = width // tile
    for k in range(CHUNKS):

        @pl.loop(k * steps // CHUNKS, (k + 1) * steps // CHUNKS)
        def _(t):
            cols = pl.ds(pl.multiple_of(t * tile, tile), tile)
            acc[:, cols] = -jnp.dot(hperm[...], down[:, cols], preferred_element_type=F32)

        if k + 1 < CHUNKS:
            gathers[k + 1] = activate(k + 1, far[k + 1])
        passes[k] = gather_pass(codes.at[k], gathers[k][0])
    for k in range(CHUNKS - 1):
        decode(k, gathers[k][1], passes[k], None)

    last = CHUNKS - 1
    for copy in [gathers[last][1]] + passes[last]:
        copy.wait_recv()
    outs.append(local(codes.at[last], codes_out.at[last]))
    dec_loads[last].wait()

    def split_sum(s):
        @pl.loop(0, sw // stile)
        def _(t):
            there = pl.ds(pl.multiple_of(t * stile, stile), stile)
            cols = pl.ds(pl.multiple_of(s * sw + t * stile, stile), stile)
            total = acc[:, cols] + jnp.dot(
                codes[last].reshape(rows, cw), dec[at_chunk(last), cols], preferred_element_type=F32
            )
            acc[:, cols] = total
            ssend[s, :, :, :, there] = total.astype(BF16).reshape(inner, outer, r16, stile)

        return [
            send(
                ssend.at[s, lax.rem(a + i, inner)],
                xrecv.at[s, i - 1],
                mp=b * inner + lax.rem(a + i, inner),
            )
            for i in range(1, inner)
        ]

    def inner_sum(s, copies):
        own = pl.ds(pl.multiple_of(a * (outer * r16), outer * r16), outer * r16)
        total = acc[own, s * sw : (s + 1) * sw].reshape(outer, r16, sw)
        for i, copy in enumerate(copies):
            copy.wait_recv()
            total = total + xrecv[s, i].astype(F32)
        zsum[s] = total
        zsend[s] = total.astype(BF16)
        return [
            send(
                zsend.at[s, lax.rem(b + i, outer)],
                zrecv.at[s, i - 1],
                mp=lax.rem(b + i, outer) * inner + a,
            )
            for i in range(1, outer)
        ]

    def outer_sum(s, copies):
        total = zsum[s, b]
        for i, copy in enumerate(copies):
            copy.wait_recv()
            total = total + zrecv[s, i].astype(F32)
        res[s, a, b] = (total + db_ref[:, s * sw : (s + 1) * sw]).astype(BF16)
        return [
            send(res.at[s, a, b], res.at[s, a, b], mp=lax.rem(b + i, outer) * inner + a)
            for i in range(1, outer)
        ]

    def inner_gather(s, copies):
        for copy in copies:
            copy.wait_recv()
        return [
            send(res.at[s, a], res.at[s, a], mp=b * inner + lax.rem(a + i, inner))
            for i in range(1, inner)
        ]

    first = [split_sum(s) for s in range(QUARTERS)]
    second = [inner_sum(s, first[s]) for s in range(QUARTERS)]
    for k in range(CHUNKS):
        for copy in [core[k]] + far[k]:
            copy.wait_send()

    back, back_far = {}, {}

    def feature_gradient(s):
        for copy in fourth[s]:
            copy.wait_recv()
        outs.append(local(res.at[s], res_out.at[s]))
        for k in range(CHUNKS):

            @pl.loop(0, cw // tile)
            def _(t):
                cols = pl.ds(pl.multiple_of(t * tile, tile), tile)
                hidden_rows = pl.ds(pl.multiple_of(k * cw + t * tile, tile), tile)
                value = lax.dot_general(
                    res[s].reshape(rows, sw),
                    dec[hidden_rows, s * sw : (s + 1) * sw],
                    (((1,), (1,)), ((), ())),
                    preferred_element_type=F32,
                )
                if s > 0:
                    value = value + part[k, :, :, cols].reshape(rows, tile)
                if s < QUARTERS - 1:
                    part[k, :, :, cols] = value.reshape(dp, rows_here, tile)
                else:
                    part_store(k, cols, value)

            if s == QUARTERS - 1:
                back[k] = send(psend.at[k, :, 1 - c], crecv.at[k], dp=partner)
                if k >= 1:
                    back_far[k - 1] = pair_sum(k - 1, back[k - 1])

    third, fourth = {}, {}
    for s in range(QUARTERS):
        third[s] = outer_sum(s, second[s])
        if s >= 1:
            fourth[s - 1] = inner_gather(s - 1, third[s - 1])
    feature_gradient(0)
    fourth[QUARTERS - 1] = inner_gather(QUARTERS - 1, third[QUARTERS - 1])
    for s in range(1, QUARTERS):
        feature_gradient(s)
    back_far[last] = pair_sum(last, back[last])
    for k in range(CHUNKS):
        cg_out[:, at_chunk(k)] = far_sum(k, back_far[k])

    for copy in tok_copies + hid_far + [hid_near] + hid_passed:
        copy.wait_send()
    for k in range(CHUNKS):
        for copy in gathers[k][0] + [gathers[k][1]] + passes[k] + [back[k]] + back_far[k]:
            copy.wait_send()
    for s in range(QUARTERS):
        for copy in first[s] + second[s] + third[s] + fourth[s]:
            copy.wait_send()
    for copy in outs:
        copy.wait()


def decoder_gradient(scale, codes_ref, res_ref, cg_ref, act_out, cg_out, out_ref):
    rows = codes_ref.shape[0] * codes_ref.shape[1]
    columns = res_ref.shape[2]
    act_out[...] = codes_ref[lax.axis_index("dp")]
    cg_out[...] = cg_ref[...]
    codes = codes_ref[...].reshape(rows, codes_ref.shape[2]).T
    for s in range(res_ref.shape[0]):
        out_ref[:, s * columns : (s + 1) * columns] = (
            jnp.dot(codes, res_ref[s], preferred_element_type=F32) * scale
        )


def on_device(
    dp,
    mp,
    tokens_in,
    gate_pre,
    up_pre,
    down_weight,
    slot_source,
    encoder,
    encoder_bias,
    decoder,
    decoder_bias,
):
    rows_here = tokens_in.shape[0]
    rows = rows_here * dp
    width, features = encoder.shape
    units = down_weight.shape[0]
    pairs = dp // 2
    inner = 1 << ((mp.bit_length() - 1) // 2)
    outer = mp // inner
    r16 = rows // mp
    cw, sw = features // CHUNKS, width // QUARTERS
    tile, stile = min(256, cw, width), min(256, sw)
    far = max(pairs - 1, 1)
    copies = (dp - 1) + 2 * (pairs - 1) * (inner - 1) + 2 * pairs - 1 + CHUNKS * (1 + pairs - 1 + 2 * pairs - 1)
    copies += QUARTERS * 2 * (inner - 1 + outer - 1) + CHUNKS * pairs
    locals_ = 1 + CHUNKS + 1 + CHUNKS + CHUNKS + QUARTERS
    vmem = pl.BlockSpec(memory_space=pltpu.VMEM)
    anywhere = pl.BlockSpec(memory_space=pl.ANY)
    code_grad, codes, res = pl.pallas_call(
        functools.partial(
            forward, (dp, pairs, inner, outer, rows_here, cw, sw, tile, stile)
        ),
        out_shape=(
            jax.ShapeDtypeStruct((rows_here, features), F32),
            jax.ShapeDtypeStruct((CHUNKS, dp, rows_here, cw), BF16),
            jax.ShapeDtypeStruct((QUARTERS, inner, outer, r16, sw), BF16),
        ),
        in_specs=[vmem, anywhere, vmem, vmem, anywhere, anywhere, vmem, anywhere, vmem],
        out_specs=(vmem, anywhere, anywhere),
        scratch_shapes=[
            pltpu.VMEM((CHUNKS, width, cw), BF16),
            pltpu.VMEM((features, width), BF16),
            pltpu.VMEM((units, width), BF16),
            pltpu.VMEM((dp, rows_here, width), BF16),
            pltpu.VMEM((rows, width), BF16),
            pltpu.VMEM((dp, rows_here, units), BF16),
            pltpu.VMEM((rows, units), BF16),
            pltpu.VMEM((CHUNKS, dp, rows_here, cw), F32),
            pltpu.VMEM((CHUNKS, pairs, 2, rows_here, cw), BF16),
            pltpu.VMEM((CHUNKS, pairs, rows_here, cw), BF16),
            pltpu.VMEM((CHUNKS, pairs, rows_here, cw), BF16),
            pltpu.VMEM((CHUNKS, far, rows_here, cw), BF16),
            pltpu.VMEM((CHUNKS, dp, rows_here, cw), BF16),
            pltpu.VMEM((rows, width), F32),
            pltpu.VMEM((QUARTERS, inner, outer, r16, sw), BF16),
            pltpu.VMEM((QUARTERS, max(inner - 1, 1), outer, r16, sw), BF16),
            pltpu.VMEM((QUARTERS, outer, r16, sw), F32),
            pltpu.VMEM((QUARTERS, outer, r16, sw), BF16),
            pltpu.VMEM((QUARTERS, max(outer - 1, 1), r16, sw), BF16),
            pltpu.VMEM((QUARTERS, inner, outer, r16, sw), BF16),
            pltpu.SemaphoreType.DMA((copies,)),
            pltpu.SemaphoreType.DMA((copies,)),
            pltpu.SemaphoreType.DMA((locals_,)),
        ],
        compiler_params=pltpu.CompilerParams(
            collective_id=0, has_side_effects=True, vmem_limit_bytes=62 * MIB
        ),
        cost_estimate=pl.CostEstimate(
            flops=2 * rows * width * (2 * features + units) + 2 * rows * width * features,
            bytes_accessed=2 * width * (2 * features + units),
            transcendentals=0,
        ),
        name="forward",
    )(
        slot_source.reshape(1, rows),
        tokens_in,
        gate_pre,
        up_pre,
        down_weight,
        encoder,
        encoder_bias.reshape(1, features),
        decoder,
        decoder_bias.reshape(1, width),
    )

    block = min(256, cw)
    per = cw // block
    here = pl.BlockSpec((rows_here, block), lambda f: (0, f))
    return pl.pallas_call(
        functools.partial(decoder_gradient, 1.0 / rows_here),
        grid=(features // block,),
        out_shape=(
            jax.ShapeDtypeStruct((rows_here, features), BF16),
            jax.ShapeDtypeStruct((rows_here, features), F32),
            jax.ShapeDtypeStruct((features, width), F32),
        ),
        in_specs=[
            pl.BlockSpec((None, dp, rows_here, block), lambda f: (f // per, 0, 0, f % per)),
            pl.BlockSpec((QUARTERS, rows, sw), lambda f: (0, 0, 0)),
            here,
        ],
        out_specs=(here, here, pl.BlockSpec((block, width), lambda f: (f, 0))),
        compiler_params=pltpu.CompilerParams(vmem_limit_bytes=62 * MIB),
        cost_estimate=pl.CostEstimate(
            flops=2 * rows * width * features,
            bytes_accessed=4 * width * features,
            transcendentals=0,
        ),
        name="decoder_gradient",
    )(codes, res.reshape(QUARTERS, rows, sw), code_grad)


def solution(mesh):
    return jax.shard_map(
        functools.partial(on_device, mesh.shape["dp"], mesh.shape["mp"]),
        mesh=mesh,
        in_specs=(
            P("dp", None),
            P("dp", "mp"),
            P("dp", "mp"),
            P("mp", "dp"),
            P(),
            P("dp", "mp"),
            P("mp"),
            P("mp", "dp"),
            P("dp"),
        ),
        out_specs=(P("dp", "mp"), P("dp", "mp"), P("mp", "dp")),
        check_vma=False,
    )
```
